32 devices in a mesh: groups: 2 (over x), tok: 16 (over z, y, core).
Axes of the slice: x: 2, y: 2, z: 4, core: 2. Of those that a mesh axis runs over, the one named last changes fastest.
Arguments:
- inputs_act: bfloat16 [2, 4096, 14336], P(None, ('groups', 'tok')), parts along dimension 1, may hold values from -6 to 6
- out_grads: bfloat16 [2, 4096, 4096], P(None, ('groups', 'tok')), parts along dimension 1, may hold values from -6 to 6
- example_ids: int32 [4096], P(('groups', 'tok')), parts along dimension 0, may hold values from 0 to 255, as said below
- proj_in: bfloat16 [14336, 64], replicated, may hold values from -0.046875 to 0.046875
- proj_out: bfloat16 [4096, 64], replicated, may hold values from -0.09375 to 0.09375
- query_sketch: bfloat16 [2, 128, 4096], P(None, ('groups', 'tok')), parts along dimension 1, may hold values from -6 to 6
- ckpt_weight: float32 [2], replicated, may hold values from 0.3 to 3
Outputs:
- scores: float32 [512, 64], P(('groups', 'tok')), parts along dimension 0
The draws below stay inside these ranges and needn't reach their ends.
There are 2 independent parts, one for each index of `groups`. The reference program is written for one: setup_inputs(seed, part) draws one part's arguments, and reference() takes and returns one part's arrays. A program takes and returns all parts, laid end to end along the dimension named above; an argument that names none is the same for every part. Nothing has to cross between parts.
Inputs may be any that keep to these rules, and one draw needn't show every extreme that they name: `example_ids`: tokens 128 * k to 128 * k + 127 name only examples 16 * k to 16 * k + 15, never falling, each of those named by at least one token.
All inputs are finite; a program needn't handle non-finite values.
Results may differ from the reference program's by a relative error of at most 0.0003.
Values may be sent and summed in bfloat16 or wider, within the bound.
No kernel may reach another device: no remote copies, remote signals or barrier semaphores. Data moves between devices by JAX's collectives and lax.ppermute only.
A program may use at most 64 MiB of HBM per device.

```python
import math
import jax
import jax.numpy as jnp
from jax import lax

D = 4096
FF = 14336
R = 64
CKPT = 2
TOK_DEV = 128
EX_DEV = 16
TOKENS = 2048
EXAMPLES = 256
NQ = 64


def draw_example_ids(key, part):
    key = jax.random.fold_in(key, 7)
    blocks = TOKENS // TOK_DEV
    extra = jax.random.randint(key, (blocks, TOK_DEV - EX_DEV), 0, EX_DEV).astype(jnp.int32)
    base = jnp.broadcast_to(jnp.arange(EX_DEV, dtype=jnp.int32), (blocks, EX_DEV))
    local = jnp.sort(jnp.concatenate([base, extra], axis=1), axis=1)
    offset = (jnp.arange(blocks, dtype=jnp.int32) * EX_DEV)[:, None]
    return (local + offset).reshape(TOKENS).astype(jnp.int32)


def block_scale(key, dims, shards, smallest, largest):
    loudness = 1.0
    for position, blocks in shards:
        heights = jax.random.uniform(jax.random.fold_in(jax.random.fold_in(key, 6), position), (blocks,), jnp.float32, smallest / len(shards), largest / len(shards))
        loudness = loudness * jnp.repeat(jnp.exp(heights), dims[position] // blocks).reshape((-1,) + (1,) * (len(dims) - 1 - position))
    return loudness


def bell_draw(rng, extent, deviation, reach, cuts=(), kind=jnp.bfloat16):
    factor_of = block_scale(rng, extent, cuts, -0.22, 0.18) if cuts else 1.0
    values = jax.random.normal(rng, extent, jnp.float32) * deviation * factor_of
    return jnp.minimum(jnp.maximum(values, -reach), reach).astype(kind)


def setup_inputs(seed: int = 0, part: int = 0) -> dict:
    streams_of = jax.random.split(jax.random.key(seed), 8)
    part_keys = jax.random.split(jax.random.fold_in(streams_of[7], part), 8)
    inputs_act = bell_draw(part_keys[0], (CKPT, TOKENS, FF), 1.0, 6.0, ((1, 16),))
    out_grads = bell_draw(part_keys[1], (CKPT, TOKENS, D), 1.0, 6.0, ((1, 16),))
    example_ids = draw_example_ids(jax.random.fold_in(jax.random.fold_in(streams_of[7], part), 71), part)
    proj_in = bell_draw(streams_of[3], (FF, R), FF ** -0.5, 0.046875)
    proj_out = bell_draw(streams_of[4], (D, R), D ** -0.5, 0.09375)
    query_sketch = bell_draw(part_keys[5], (CKPT, NQ, R * R), 1.0, 6.0, ((1, 16),))
    ckpt_weight = jnp.clip(jnp.exp(jax.random.uniform(streams_of[6], (CKPT,), jnp.float32, math.log(0.3), math.log(3.0))), 0.3, 3.0)
    return {"inputs_act": inputs_act, "out_grads": out_grads, "example_ids": example_ids, "proj_in": proj_in, "proj_out": proj_out, "query_sketch": query_sketch, "ckpt_weight": ckpt_weight}


def damped_inverse(factor):
    size = factor.shape[0]
    eye = jnp.eye(size, dtype=jnp.float32)
    damped = factor + 0.05 * (jnp.trace(factor) / size) * eye
    lower = jnp.linalg.cholesky(damped)
    return jax.scipy.linalg.cho_solve((lower, True), eye)

def reference(inputs_act, out_grads, example_ids, proj_in, proj_out, query_sketch, ckpt_weight):
    scores = jnp.zeros((EXAMPLES, NQ), jnp.float32)
    for step in range(CKPT):
        act_side = jnp.dot(inputs_act[step].astype(jnp.float32), proj_in.astype(jnp.float32), preferred_element_type=jnp.float32)
        grad_side = jnp.dot(out_grads[step].astype(jnp.float32), proj_out.astype(jnp.float32), preferred_element_type=jnp.float32)
        fact_a = jnp.dot(act_side.T, act_side, precision=lax.Precision.HIGHEST) / TOKENS
        fact_s = jnp.dot(grad_side.T, grad_side, precision=lax.Precision.HIGHEST) / TOKENS
        inv_a = damped_inverse(fact_a)
        inv_s = damped_inverse(fact_s)
        outer = (grad_side[:, :, None] * act_side[:, None, :]).reshape(TOKENS, R * R)
        sketch = jax.ops.segment_sum(outer, example_ids, num_segments=EXAMPLES)
        queries = query_sketch[step].astype(jnp.float32).reshape(NQ, R, R)
        prec = jnp.einsum('ij,qjk,kl->qil', inv_s, queries, inv_a, precision=lax.Precision.HIGHEST)
        prec = prec.reshape(NQ, R * R)
        inner = jnp.dot(sketch, prec.T, precision=lax.Precision.HIGHEST)
        scores = scores + ckpt_weight[step] / R * inner
    return scores
```

```python
import functools

import jax
import jax.numpy as jnp
from jax import lax
from jax.experimental import pallas as pl
from jax.experimental.pallas import tpu as pltpu
from jax.sharding import PartitionSpec as P

EX_DEV = 16
HIGH = lax.Precision.HIGHEST
F32 = jnp.float32
BF16 = jnp.bfloat16
VMEM = pl.BlockSpec(memory_space=pltpu.VMEM)
ANY = pl.BlockSpec(memory_space=pl.ANY)


def nt(x, y, precision=None):
    return lax.dot_general(
        x, y, (((1,), (1,)), ((), ())), precision=precision, preferred_element_type=F32
    )


def project_kernel(chunks, act, grad, ids, pin, pout, keep, send, act_v, grad_v, pin_v, pout_v, sems):
    ckpts, rows, depth = act.shape
    side = pin.shape[0]
    step = depth // chunks
    copies = [
        pltpu.make_async_copy(pout, pout_v, sems.at[0]),
        pltpu.make_async_copy(grad, grad_v, sems.at[1]),
    ]
    for k in range(chunks):
        span = pl.ds(k * step, step)
        copies.append(pltpu.make_async_copy(pin.at[:, span], pin_v.at[:, span], sems.at[2 + 2 * k]))
        copies.append(
            pltpu.make_async_copy(act.at[:, :, span], act_v.at[:, :, span], sems.at[3 + 2 * k])
        )
    for copy in copies:
        copy.start()
    copies[0].wait()
    copies[1].wait()
    s = nt(grad_v[...].reshape(ckpts * rows, -1), pout_v[...])
    a = jnp.zeros((ckpts * rows, side), F32)
    for k in range(chunks):
        copies[2 + 2 * k].wait()
        copies[3 + 2 * k].wait()
        span = slice(k * step, (k + 1) * step)
        a = a + nt(act_v[:, :, span].reshape(ckpts * rows, step), pin_v[:, span])
    both = jnp.concatenate([a, s], axis=1)
    odd = lax.rem(lax.axis_index("tok"), 2)
    first, second = both[:rows], both[rows:]
    keep[...] = jnp.where(odd == 0, first, second)
    send[0:rows, :] = jnp.where(odd == 0, second, first)
    send[rows : rows + 8, :] = jnp.broadcast_to(ids[...].astype(F32), (8, rows))


def project(act, grad, ids, pin, pout):
    ckpts, rows, depth = act.shape
    side, width = pout.shape
    chunks = 8
    return pl.pallas_call(
        functools.partial(project_kernel, chunks),
        out_shape=(
            jax.ShapeDtypeStruct((rows, 2 * side), F32),
            jax.ShapeDtypeStruct((rows + 8, 2 * side), F32),
        ),
        in_specs=[ANY, ANY, VMEM, ANY, ANY],
        out_specs=(VMEM, VMEM),
        scratch_shapes=[
            pltpu.VMEM((ckpts, rows, depth), BF16),
            pltpu.VMEM((ckpts, rows, width), BF16),
            pltpu.VMEM((side, depth), BF16),
            pltpu.VMEM((side, width), BF16),
            pltpu.SemaphoreType.DMA((2 + 2 * chunks,)),
        ],
        compiler_params=pltpu.CompilerParams(vmem_limit_bytes=40 * 2**20),
        name="project",
    )(act, grad, ids, pin, pout)


def factor_kernel(total, mine, other, out):
    rows, lanes = mine.shape
    side = lanes // 2
    x = jnp.concatenate([mine[...], other[0:rows, :]], axis=0)
    g = lax.dot_general(
        x, x, (((0,), (0,)), ((), ())), precision=HIGH, preferred_element_type=F32
    )
    lane = lax.broadcasted_iota(jnp.int32, (side, lanes), 1)
    out[...] = jnp.where(lane < side, g[:side], g[side:]) * (1.0 / total)


def inverse_kernel(g, out):
    side, lanes = g.shape
    lane = lax.broadcasted_iota(jnp.int32, (side, lanes), 1)
    row = lax.broadcasted_iota(jnp.int32, (side, lanes), 0)
    left = lane < side
    local = jnp.where(left, lane, lane - side)
    m = g[...]
    diag = jnp.sum(jnp.where(local == row, m, 0.0), axis=0, keepdims=True)
    lead = left[:1]
    tr_a = jnp.sum(jnp.where(lead, diag, 0.0), axis=1, keepdims=True)
    tr_s = jnp.sum(jnp.where(lead, 0.0, diag), axis=1, keepdims=True)
    damp = 0.05 * (jnp.where(lead, tr_a, tr_s) / side)
    m = m + jnp.where(local == row, damp, 0.0)
    for k in range(side):
        col = jnp.where(left, m[:, k : k + 1], m[:, side + k : side + k + 1])
        pivot = 1.0 / col[k : k + 1]
        mark = local[:1] == k
        line = jnp.where(mark, 1.0, m[k : k + 1]) * pivot
        here = row == k
        m = jnp.where(here, 0.0, jnp.where(local == k, 0.0, m)) - jnp.where(here, -1.0, col) * line
    out[...] = m


def split(x):
    hi = x.astype(BF16)
    return hi, (x - hi.astype(F32)).astype(BF16)


def score_kernel(q_rows, masks, inv, mine, other, ids, queries, weight, keep, send):
    rows, lanes = mine.shape
    side = lanes // 2
    ckpt = lax.rem(lax.axis_index("tok"), 2)
    me = lax.axis_index("tok")
    x = jnp.concatenate([mine[...], other[0:rows, :]], axis=0)
    lane = lax.broadcasted_iota(jnp.int32, (side, lanes), 1)
    left = lane < side
    p = inv[...]
    ai = jnp.where(left, p, pltpu.roll(p, side, 1))
    si = jnp.where(left, 0.0, p)
    aa = jnp.dot(
        x,
        jnp.concatenate([ai, jnp.zeros_like(ai)], axis=0),
        precision=HIGH,
        preferred_element_type=F32,
    )
    st = nt(si, x, HIGH)
    a_hi, a_lo = split(aa)
    s_hi, s_lo = split(st)
    s_hi, s_lo = s_hi.astype(F32), s_lo.astype(F32)
    example = lax.broadcasted_iota(jnp.int32, (EX_DEV, rows), 0)
    own_ids = ids[...] - me * EX_DEV
    near = me + 1 - 2 * ckpt
    far_ids = other[rows : rows + 1, :].astype(jnp.int32) - near * EX_DEV
    parts = []
    for block, which in enumerate((own_ids, far_ids)):
        mask = (which == example).astype(F32)
        span = slice(block * rows, (block + 1) * rows)
        lhs = jnp.concatenate(
            [
                (v[:, None, span] * mask[None]).reshape(side * EX_DEV, rows).astype(BF16)
                for v in (s_hi, s_lo)
            ],
            axis=1,
        )
        rhs = jnp.concatenate(
            [
                jnp.concatenate([a_hi[span], a_lo[span]], axis=1),
                jnp.concatenate([a_hi[span], jnp.zeros_like(a_lo[span])], axis=1),
            ],
            axis=0,
        )
        both = jnp.dot(lhs, rhs, preferred_element_type=F32)
        both = (both[:, :lanes] + both[:, lanes:]).reshape(side // 2, 2, EX_DEV, lanes)
        first = lax.broadcasted_iota(jnp.int32, (EX_DEV, lanes), 1) < side
        parts.append(
            jnp.concatenate(
                [jnp.where(first, both[j, 0], both[j, 1]) for j in range(side // 2)], axis=1
            )
        )
    sketch = jnp.concatenate(parts, axis=0)
    k_hi, k_lo = split(sketch)
    inner = nt(jnp.concatenate([k_hi, k_lo], axis=0), queries[...])
    inner = inner[: 2 * EX_DEV] + inner[2 * EX_DEV :]
    count = queries.shape[0]
    src = lax.broadcasted_iota(jnp.int32, (count, count), 0)
    dst = lax.broadcasted_iota(jnp.int32, (count, count), 1)
    shift = q_rows.bit_length() - 1
    block = me
    for bit, mask in enumerate(masks):
        block = block ^ ((src >> (shift + bit)) & 1) * mask
    order = (block * q_rows + (src & (q_rows - 1)) == dst).astype(F32)
    scores = jnp.dot(inner, order, precision=HIGH, preferred_element_type=F32)
    scores = scores * (weight[ckpt] / side)
    keep[...] = scores[:EX_DEV]
    send[...] = scores[EX_DEV:]


def local(inputs_act, out_grads, example_ids, proj_in, proj_out, query_sketch, ckpt_weight):
    rows = inputs_act.shape[1]
    side = proj_in.shape[1]
    q_rows = query_sketch.shape[1]
    devices = lax.axis_size("tok")
    total = rows * devices
    me = lax.axis_index("tok")

    def swap(x, mask):
        return lax.ppermute(x, "tok", [(i, i ^ mask) for i in range(devices)])

    ids = example_ids.reshape(1, rows)
    even = lax.rem(me, 2) == 0
    q_keep = jnp.where(even, query_sketch[0], query_sketch[1])
    q_send = jnp.where(even, query_sketch[1], query_sketch[0])
    mine, send = project(inputs_act, out_grads, ids, proj_in.T, proj_out.T)
    other = swap(send, 1)
    queries = jnp.concatenate([q_keep, swap(q_send, 1)], axis=0)
    g = pl.pallas_call(
        functools.partial(factor_kernel, total),
        out_shape=jax.ShapeDtypeStruct((side, 2 * side), F32),
        in_specs=[VMEM, VMEM],
        out_specs=VMEM,
        name="factor",
    )(mine, other)
    masks = [1]
    while devices >> len(masks) > 1:
        masks.append(devices >> len(masks))
    for mask in masks[1:]:
        g = g + swap(g, mask)
        queries = jnp.concatenate([queries, swap(queries, mask)], axis=0)
    inv = pl.pallas_call(
        inverse_kernel,
        out_shape=jax.ShapeDtypeStruct((side, 2 * side), F32),
        in_specs=[VMEM],
        out_specs=VMEM,
        name="inverse",
    )(g)
    keep, send = pl.pallas_call(
        functools.partial(score_kernel, q_rows, tuple(masks)),
        out_shape=(
            jax.ShapeDtypeStruct((EX_DEV, q_rows * devices), F32),
            jax.ShapeDtypeStruct((EX_DEV, q_rows * devices), F32),
        ),
        in_specs=[VMEM] * 5 + [pl.BlockSpec(memory_space=pltpu.SMEM)],
        out_specs=(VMEM, VMEM),
        compiler_params=pltpu.CompilerParams(vmem_limit_bytes=40 * 2**20),
        name="score",
    )(inv, mine, other, ids, queries, ckpt_weight)
    return keep + swap(send, 1)


def solution(mesh):
    return jax.shard_map(
        local,
        mesh=mesh,
        in_specs=(
            P(None, ("groups", "tok"), None),
            P(None, ("groups", "tok"), None),
            P(("groups", "tok")),
            P(),
            P(),
            P(None, ("groups", "tok"), None),
            P(),
        ),
        out_specs=P(("groups", "tok"), None),
        check_vma=False,
    )
```

```python
import functools

import jax
import jax.numpy as jnp
from jax import lax
from jax.experimental import pallas as pl
from jax.experimental.pallas import tpu as pltpu
from jax.sharding import PartitionSpec as P

EX_DEV = 16
HIGH = lax.Precision.HIGHEST
F32 = jnp.float32
BF16 = jnp.bfloat16
VMEM = pl.BlockSpec(memory_space=pltpu.VMEM)
HBM = pl.BlockSpec(memory_space=pltpu.HBM)


def nt(x, y, precision=None):
    return lax.dot_general(
        x, y, (((1,), (1,)), ((), ())), precision=precision, preferred_element_type=F32
    )


def project_kernel(
    chunks, act, grad, ids, pin, pout, query, weight,
    keep, send, q_keep, q_send,
    act_v, grad_v, ids_v, pin_v, pout_v, query_v, weight_v, sems,
):
    ckpts, rows, depth = act.shape
    side = pin.shape[0]
    step = depth // chunks
    copies = [
        pltpu.make_async_copy(pout, pout_v, sems.at[0]),
        pltpu.make_async_copy(grad, grad_v, sems.at[1]),
        pltpu.make_async_copy(query, query_v, sems.at[2]),
        pltpu.make_async_copy(ids, ids_v, sems.at[3]),
        pltpu.make_async_copy(weight, weight_v, sems.at[4]),
    ]
    for k in range(chunks):
        span = pl.ds(k * step, step)
        copies.append(pltpu.make_async_copy(pin.at[:, span], pin_v.at[:, span], sems.at[5 + 2 * k]))
        copies.append(
            pltpu.make_async_copy(act.at[:, :, span], act_v.at[:, :, span], sems.at[6 + 2 * k])
        )
    for copy in copies:
        copy.start()
    for copy in copies[:5]:
        copy.wait()
    odd = lax.rem(lax.axis_index("tok"), 2)
    tail = jnp.broadcast_to(ids_v[...].astype(F32), (8, rows))
    keep[rows : rows + 8, :] = tail
    send[rows : rows + 8, :] = tail
    keep[rows + 8 :, :] = jnp.full((8, 2 * side), weight_v[odd] / side, F32)
    q_keep[...] = jnp.where(odd == 0, query_v[0], query_v[1])
    q_send[...] = jnp.where(odd == 0, query_v[1], query_v[0])
    s = nt(grad_v[...].reshape(ckpts * rows, -1), pout_v[...])
    a = jnp.zeros((ckpts * rows, side), F32)
    for k in range(chunks):
        copies[5 + 2 * k].wait()
        copies[6 + 2 * k].wait()
        span = slice(k * step, (k + 1) * step)
        a = a + nt(act_v[:, :, span].reshape(ckpts * rows, step), pin_v[:, span])
    both = jnp.concatenate([a, s], axis=1)
    first, second = both[:rows], both[rows:]
    keep[0:rows, :] = jnp.where(odd == 0, first, second)
    send[0:rows, :] = jnp.where(odd == 0, second, first)


def project(act, grad, ids, pin, pout, query, weight):
    ckpts, rows, depth = act.shape
    side, width = pout.shape
    chunks = 8
    return pl.pallas_call(
        functools.partial(project_kernel, chunks),
        out_shape=(
            jax.ShapeDtypeStruct((rows + 16, 2 * side), F32),
            jax.ShapeDtypeStruct((rows + 8, 2 * side), F32),
            jax.ShapeDtypeStruct(query.shape[1:], BF16),
            jax.ShapeDtypeStruct(query.shape[1:], BF16),
        ),
        in_specs=[HBM] * 7,
        out_specs=(VMEM,) * 4,
        scratch_shapes=[
            pltpu.VMEM((ckpts, rows, depth), BF16),
            pltpu.VMEM((ckpts, rows, width), BF16),
            pltpu.VMEM((1, rows), jnp.int32),
            pltpu.VMEM((side, depth), BF16),
            pltpu.VMEM((side, width), BF16),
            pltpu.VMEM(query.shape, BF16),
            pltpu.SMEM(weight.shape, F32),
            pltpu.SemaphoreType.DMA((5 + 2 * chunks,)),
        ],
        compiler_params=pltpu.CompilerParams(vmem_limit_bytes=63 * 2**20),
        name="project",
    )(act, grad, ids, pin, pout, query, weight)


def factor_kernel(total, mine, other, out):
    rows, lanes = other.shape[0] - 8, other.shape[1]
    side = lanes // 2
    x = jnp.concatenate([mine[0:rows, :], other[0:rows, :]], axis=0)
    g = lax.dot_general(
        x, x, (((0,), (0,)), ((), ())), precision=HIGH, preferred_element_type=F32
    )
    lane = lax.broadcasted_iota(jnp.int32, (side, lanes), 1)
    out[...] = jnp.where(lane < side, g[:side], g[side:]) * (1.0 / total)


def inverse_kernel(g, out):
    side, lanes = g.shape
    lane = lax.broadcasted_iota(jnp.int32, (side, lanes), 1)
    row = lax.broadcasted_iota(jnp.int32, (side, lanes), 0)
    left = lane < side
    local = jnp.where(left, lane, lane - side)
    m = g[...]
    diag = jnp.sum(jnp.where(local == row, m, 0.0), axis=0, keepdims=True)
    lead = left[:1]
    tr_a = jnp.sum(jnp.where(lead, diag, 0.0), axis=1, keepdims=True)
    tr_s = jnp.sum(jnp.where(lead, 0.0, diag), axis=1, keepdims=True)
    damp = 0.05 * (jnp.where(lead, tr_a, tr_s) / side)
    m = m + jnp.where(local == row, damp, 0.0)
    for k in range(side):
        col = jnp.where(left, m[:, k : k + 1], m[:, side + k : side + k + 1])
        pivot = 1.0 / col[k : k + 1]
        mark = local[:1] == k
        line = jnp.where(mark, 1.0, m[k : k + 1]) * pivot
        here = row == k
        m = jnp.where(here, 0.0, jnp.where(local == k, 0.0, m)) - jnp.where(here, -1.0, col) * line
    out[...] = m


def split(x):
    hi = x.astype(BF16)
    return hi, (x - hi.astype(F32)).astype(BF16)


def score_kernel(q_rows, masks, inv, mine, other, queries, keep, send):
    rows, lanes = other.shape[0] - 8, other.shape[1]
    side = lanes // 2
    ckpt = lax.rem(lax.axis_index("tok"), 2)
    me = lax.axis_index("tok")
    x = jnp.concatenate([mine[0:rows, :], other[0:rows, :]], axis=0)
    lane = lax.broadcasted_iota(jnp.int32, (side, lanes), 1)
    left = lane < side
    p = inv[...]
    ai = jnp.where(left, p, pltpu.roll(p, side, 1))
    si = jnp.where(left, 0.0, p)
    aa = jnp.dot(
        x,
        jnp.concatenate([ai, jnp.zeros_like(ai)], axis=0),
        precision=HIGH,
        preferred_element_type=F32,
    )
    st = nt(si, x, HIGH)
    a_hi, a_lo = split(aa)
    s_hi, s_lo = split(st)
    s_hi, s_lo = s_hi.astype(F32), s_lo.astype(F32)
    example = lax.broadcasted_iota(jnp.int32, (EX_DEV, rows), 0)
    own_ids = mine[rows : rows + 1, :].astype(jnp.int32) - me * EX_DEV
    near = me + 1 - 2 * ckpt
    far_ids = other[rows : rows + 1, :].astype(jnp.int32) - near * EX_DEV
    parts = []
    for block, which in enumerate((own_ids, far_ids)):
        mask = (which == example).astype(F32)
        span = slice(block * rows, (block + 1) * rows)
        lhs = jnp.concatenate(
            [
                (v[:, None, span] * mask[None]).reshape(side * EX_DEV, rows).astype(BF16)
                for v in (s_hi, s_lo)
            ],
            axis=1,
        )
        rhs = jnp.concatenate(
            [
                jnp.concatenate([a_hi[span], a_lo[span]], axis=1),
                jnp.concatenate([a_hi[span], jnp.zeros_like(a_lo[span])], axis=1),
            ],
            axis=0,
        )
        both = jnp.dot(lhs, rhs, preferred_element_type=F32)
        both = (both[:, :lanes] + both[:, lanes:]).reshape(side // 2, 2, EX_DEV, lanes)
        first = lax.broadcasted_iota(jnp.int32, (EX_DEV, lanes), 1) < side
        parts.append(
            jnp.concatenate(
                [jnp.where(first, both[j, 0], both[j, 1]) for j in range(side // 2)], axis=1
            )
        )
    sketch = jnp.concatenate(parts, axis=0)
    k_hi, k_lo = split(sketch)
    inner = nt(jnp.concatenate([k_hi, k_lo], axis=0), queries[...])
    inner = inner[: 2 * EX_DEV] + inner[2 * EX_DEV :]
    count = queries.shape[0]
    src = lax.broadcasted_iota(jnp.int32, (count, count), 0)
    dst = lax.broadcasted_iota(jnp.int32, (count, count), 1)
    shift = q_rows.bit_length() - 1
    block = me
    for bit, mask in enumerate(masks):
        block = block ^ ((src >> (shift + bit)) & 1) * mask
    order = (block * q_rows + (src & (q_rows - 1)) == dst).astype(F32)
    scores = jnp.dot(inner, order, precision=HIGH, preferred_element_type=F32)
    scores = scores * mine[rows + 8 : rows + 9, 0:1]
    keep[...] = scores[:EX_DEV]
    send[...] = scores[EX_DEV:]


def local(inputs_act, out_grads, example_ids, proj_in, proj_out, query_sketch, ckpt_weight):
    rows = inputs_act.shape[1]
    side = proj_in.shape[1]
    q_rows = query_sketch.shape[1]
    devices = lax.axis_size("tok")
    total = rows * devices
    me = lax.axis_index("tok")

    def swap(x, mask):
        return lax.ppermute(x, "tok", [(i, i ^ mask) for i in range(devices)])

    ids = example_ids.reshape(1, rows)
    mine, send, q_keep, q_send = project(
        inputs_act, out_grads, ids, proj_in.T, proj_out.T, query_sketch, ckpt_weight
    )
    other = swap(send, 1)
    queries = jnp.concatenate([q_keep, swap(q_send, 1)], axis=0)
    g = pl.pallas_call(
        functools.partial(factor_kernel, total),
        out_shape=jax.ShapeDtypeStruct((side, 2 * side), F32),
        in_specs=[VMEM, VMEM],
        out_specs=VMEM,
        compiler_params=pltpu.CompilerParams(vmem_limit_bytes=4 * 2**20),
        name="factor",
    )(mine, other)
    masks = [1]
    while devices >> len(masks) > 1:
        masks.append(devices >> len(masks))
    for mask in masks[1:]:
        queries, _ = lax.optimization_barrier((queries, g))
        g = g + swap(g, mask)
        queries = jnp.concatenate([queries, swap(queries, mask)], axis=0)
    inv = pl.pallas_call(
        inverse_kernel,
        out_shape=jax.ShapeDtypeStruct((side, 2 * side), F32),
        in_specs=[VMEM],
        out_specs=VMEM,
        compiler_params=pltpu.CompilerParams(vmem_limit_bytes=4 * 2**20),
        name="inverse",
    )(g)
    keep, send = pl.pallas_call(
        functools.partial(score_kernel, q_rows, tuple(masks)),
        out_shape=(
            jax.ShapeDtypeStruct((EX_DEV, q_rows * devices), F32),
            jax.ShapeDtypeStruct((EX_DEV, q_rows * devices), F32),
        ),
        in_specs=[VMEM] * 4,
        out_specs=(VMEM, VMEM),
        compiler_params=pltpu.CompilerParams(vmem_limit_bytes=16 * 2**20),
        name="score",
    )(inv, mine, other, queries)
    return keep + swap(send, 1)


def solution(mesh):
    return jax.shard_map(
        local,
        mesh=mesh,
        in_specs=(
            P(None, ("groups", "tok"), None),
            P(None, ("groups", "tok"), None),
            P(("groups", "tok")),
            P(),
            P(),
            P(None, ("groups", "tok"), None),
            P(),
        ),
        out_specs=P(("groups", "tok"), None),
        check_vma=False,
    )
```

```python
import functools

import jax
import jax.numpy as jnp
from jax import lax
from jax.experimental import pallas as pl
from jax.experimental.pallas import tpu as pltpu
from jax.sharding import PartitionSpec as P

EX_DEV = 16
BLOCK = 8
LIGHT, HEAVY = 10**6, 2 * 10**10
HIGH = lax.Precision.HIGHEST
F32 = jnp.float32
BF16 = jnp.bfloat16
VMEM = pl.BlockSpec(memory_space=pltpu.VMEM)
HBM = pl.BlockSpec(memory_space=pltpu.HBM)


def nt(x, y, precision=None):
    return lax.dot_general(
        x, y, (((1,), (1,)), ((), ())), precision=precision, preferred_element_type=F32
    )


def project_kernel(
    chunks, act, grad, ids, pin, pout, weight,
    keep, send,
    act_v, grad_v, ids_v, pin_v, pout_v, weight_v, sems,
):
    ckpts, rows, depth = act.shape
    side = pin.shape[0]
    step = depth // chunks
    copies = [
        pltpu.make_async_copy(pout, pout_v, sems.at[0]),
        pltpu.make_async_copy(grad, grad_v, sems.at[1]),
        pltpu.make_async_copy(ids, ids_v, sems.at[2]),
        pltpu.make_async_copy(weight, weight_v, sems.at[3]),
    ]
    for k in range(chunks):
        span = pl.ds(k * step, step)
        copies.append(pltpu.make_async_copy(pin.at[:, span], pin_v.at[:, span], sems.at[4 + 2 * k]))
        copies.append(
            pltpu.make_async_copy(act.at[:, :, span], act_v.at[:, :, span], sems.at[5 + 2 * k])
        )
    for copy in copies:
        copy.start()
    for copy in copies[:4]:
        copy.wait()
    odd = lax.rem(lax.axis_index("tok"), 2)
    tail = jnp.broadcast_to(ids_v[...].astype(F32), (8, rows))
    keep[rows : rows + 8, :] = tail
    send[rows : rows + 8, :] = tail
    keep[rows + 8 :, :] = jnp.full((8, 2 * side), weight_v[odd] / side, F32)
    s = nt(grad_v[...].reshape(ckpts * rows, -1), pout_v[...])
    a = jnp.zeros((ckpts * rows, side), F32)
    for k in range(chunks):
        copies[4 + 2 * k].wait()
        copies[5 + 2 * k].wait()
        span = slice(k * step, (k + 1) * step)
        a = a + nt(act_v[:, :, span].reshape(ckpts * rows, step), pin_v[:, span])
    both = jnp.concatenate([a, s], axis=1)
    first, second = both[:rows], both[rows:]
    keep[0:rows, :] = jnp.where(odd == 0, first, second)
    send[0:rows, :] = jnp.where(odd == 0, second, first)


def project(act, grad, ids, pin, pout, weight):
    ckpts, rows, depth = act.shape
    side, width = pout.shape
    chunks = 8
    return pl.pallas_call(
        functools.partial(project_kernel, chunks),
        out_shape=(
            jax.ShapeDtypeStruct((rows + 16, 2 * side), F32),
            jax.ShapeDtypeStruct((rows + 8, 2 * side), F32),
        ),
        in_specs=[HBM] * 6,
        out_specs=(VMEM, VMEM),
        scratch_shapes=[
            pltpu.VMEM((ckpts, rows, depth), BF16),
            pltpu.VMEM((ckpts, rows, width), BF16),
            pltpu.VMEM((1, rows), jnp.int32),
            pltpu.VMEM((side, depth), BF16),
            pltpu.VMEM((side, width), BF16),
            pltpu.SMEM(weight.shape, F32),
            pltpu.SemaphoreType.DMA((4 + 2 * chunks,)),
        ],
        compiler_params=pltpu.CompilerParams(vmem_limit_bytes=63 * 2**20),
        cost_estimate=pl.CostEstimate(flops=HEAVY, bytes_accessed=2 * 10**7, transcendentals=0),
        name="project",
    )(act, grad, ids, pin, pout, weight)


def gram_kernel(total, rows, x, *rest):
    lanes = x.shape[1]
    side = lanes // 2
    x = x[0:rows, :]
    g = lax.dot_general(
        x, x, (((0,), (0,)), ((), ())), precision=HIGH, preferred_element_type=F32
    )
    lane = lax.broadcasted_iota(jnp.int32, (side, lanes), 1)
    g = jnp.where(lane < side, g[:side], g[side:]) * (1.0 / total)
    for more in rest[:-1]:
        g = g + more[...]
    rest[-1][...] = g


def gram(total, rows, cost, x, *more):
    lanes = x.shape[1]
    return pl.pallas_call(
        functools.partial(gram_kernel, total, rows),
        out_shape=jax.ShapeDtypeStruct((lanes // 2, lanes), F32),
        in_specs=[VMEM] * (1 + len(more)),
        out_specs=VMEM,
        compiler_params=pltpu.CompilerParams(vmem_limit_bytes=4 * 2**20),
        cost_estimate=pl.CostEstimate(flops=cost, bytes_accessed=cost // 1000, transcendentals=0),
        name="gram",
    )(x, *more)


def tick_kernel(*refs):
    total = refs[0][...]
    for ref in refs[1:-1]:
        total = total + ref[...]
    refs[-1][...] = total


def tick(weight, *terms):
    return pl.pallas_call(
        tick_kernel,
        out_shape=jax.ShapeDtypeStruct(terms[0].shape, F32),
        in_specs=[VMEM] * len(terms),
        out_specs=VMEM,
        compiler_params=pltpu.CompilerParams(vmem_limit_bytes=2**20),
        cost_estimate=pl.CostEstimate(
            flops=weight, bytes_accessed=weight // 1000, transcendentals=0
        ),
        name="tick",
    )(*terms)


def inverse_kernel(g, out):
    side, lanes = g.shape
    lane = lax.broadcasted_iota(jnp.int32, (side, lanes), 1)
    row = lax.broadcasted_iota(jnp.int32, (side, lanes), 0)
    left = lane < side
    local = jnp.where(left, lane, lane - side)
    m = g[...]
    diag = jnp.sum(jnp.where(local == row, m, 0.0), axis=0, keepdims=True)
    first = left[:1]
    tr_a = jnp.sum(jnp.where(first, diag, 0.0), axis=1, keepdims=True)
    tr_s = jnp.sum(jnp.where(first, 0.0, diag), axis=1, keepdims=True)
    damp = 0.05 * (jnp.where(first, tr_a, tr_s) / side)
    m = m + jnp.where(local == row, damp, 0.0)
    lead = local[:1]
    for k in range(0, side, BLOCK):
        at = jnp.where(left, k, side + k)
        cols = [jnp.take_along_axis(m, at + j, axis=1) for j in range(BLOCK)]
        small = [[col[k + i : k + i + 1] for col in cols] for i in range(BLOCK)]
        lines = []
        for i in range(BLOCK):
            line = m[k + i : k + i + 1]
            for j in range(BLOCK):
                line = jnp.where(lead == k + j, float(i == j), line)
            lines.append(line)
        for p in range(BLOCK):
            scale = 1.0 / small[p][p]
            for j in range(p + 1, BLOCK):
                small[p][j] = small[p][j] * scale
            lines[p] = lines[p] * scale
            for i in range(BLOCK):
                if i != p:
                    factor = small[i][p]
                    for j in range(p + 1, BLOCK):
                        small[i][j] = small[i][j] - factor * small[p][j]
                    lines[i] = lines[i] - factor * lines[p]
        inside = (row >= k) & (row < k + BLOCK)
        m = jnp.where(inside | ((local >= k) & (local < k + BLOCK)), 0.0, m)
        for j in range(BLOCK):
            m = m - jnp.where(row == k + j, -1.0, jnp.where(inside, 0.0, cols[j])) * lines[j]
    out[...] = m


def split(x):
    hi = x.astype(BF16)
    return hi, (x - hi.astype(F32)).astype(BF16)


def score_kernel(q_rows, masks, inv, mine, other, queries, keep, send):
    rows, lanes = other.shape[0] - 8, other.shape[1]
    side = lanes // 2
    ckpt = lax.rem(lax.axis_index("tok"), 2)
    me = lax.axis_index("tok")
    x = jnp.concatenate([mine[0:rows, :], other[0:rows, :]], axis=0)
    lane = lax.broadcasted_iota(jnp.int32, (side, lanes), 1)
    left = lane < side
    p = inv[...]
    ai = jnp.where(left, p, pltpu.roll(p, side, 1))
    si = jnp.where(left, 0.0, p)
    aa = jnp.dot(
        x,
        jnp.concatenate([ai, jnp.zeros_like(ai)], axis=0),
        precision=HIGH,
        preferred_element_type=F32,
    )
    st = nt(si, x, HIGH)
    a_hi, a_lo = split(aa)
    s_hi, s_lo = split(st)
    s_hi, s_lo = s_hi.astype(F32), s_lo.astype(F32)
    example = lax.broadcasted_iota(jnp.int32, (EX_DEV, rows), 0)
    own_ids = mine[rows : rows + 1, :].astype(jnp.int32) - me * EX_DEV
    near = me + 1 - 2 * ckpt
    far_ids = other[rows : rows + 1, :].astype(jnp.int32) - near * EX_DEV
    parts = []
    for block, which in enumerate((own_ids, far_ids)):
        mask = (which == example).astype(F32)
        span = slice(block * rows, (block + 1) * rows)
        lhs = jnp.concatenate(
            [
                (v[:, None, span] * mask[None]).reshape(side * EX_DEV, rows).astype(BF16)
                for v in (s_hi, s_lo)
            ],
            axis=1,
        )
        rhs = jnp.concatenate(
            [
                jnp.concatenate([a_hi[span], a_lo[span]], axis=1),
                jnp.concatenate([a_hi[span], jnp.zeros_like(a_lo[span])], axis=1),
            ],
            axis=0,
        )
        both = jnp.dot(lhs, rhs, preferred_element_type=F32)
        both = (both[:, :lanes] + both[:, lanes:]).reshape(side // 2, 2, EX_DEV, lanes)
        first = lax.broadcasted_iota(jnp.int32, (EX_DEV, lanes), 1) < side
        parts.append(
            jnp.concatenate(
                [jnp.where(first, both[j, 0], both[j, 1]) for j in range(side // 2)], axis=1
            )
        )
    sketch = jnp.concatenate(parts, axis=0)
    k_hi, k_lo = split(sketch)
    inner = nt(jnp.concatenate([k_hi, k_lo], axis=0), queries[...])
    inner = inner[: 2 * EX_DEV] + inner[2 * EX_DEV :]
    count = queries.shape[0]
    src = lax.broadcasted_iota(jnp.int32, (count, count), 0)
    dst = lax.broadcasted_iota(jnp.int32, (count, count), 1)
    shift = q_rows.bit_length() - 1
    block = me
    for bit, mask in enumerate(masks):
        block = block ^ ((src >> (shift + bit)) & 1) * mask
    order = (block * q_rows + (src & (q_rows - 1)) == dst).astype(F32)
    scores = jnp.dot(inner, order, precision=HIGH, preferred_element_type=F32)
    scores = scores * mine[rows + 8 : rows + 9, 0:1]
    keep[...] = scores[:EX_DEV]
    send[...] = scores[EX_DEV:]


def local(inputs_act, out_grads, example_ids, proj_in, proj_out, query_sketch, ckpt_weight):
    rows = inputs_act.shape[1]
    side = proj_in.shape[1]
    q_rows = query_sketch.shape[1]
    devices = lax.axis_size("tok")
    total = rows * devices
    me = lax.axis_index("tok")

    def swap(x, mask):
        return lax.ppermute(x, "tok", [(i, i ^ mask) for i in range(devices)])

    ids = example_ids.reshape(1, rows)
    first = devices // 2
    arrived = swap(query_sketch, first)
    mine, send = project(inputs_act, out_grads, ids, proj_in.T, proj_out.T, ckpt_weight)
    other = swap(send, 1)
    arrived, mine = lax.optimization_barrier((arrived, mine))
    both = jnp.concatenate([query_sketch, arrived], axis=1)
    even = lax.rem(me, 2) == 0
    queries = jnp.where(even, both[0], both[1])
    queries = jnp.concatenate([queries, swap(jnp.where(even, both[1], both[0]), 1)], axis=0)
    g = gram(total, rows, LIGHT, other, gram(total, rows, HEAVY, mine))
    sums = [first]
    while sums[-1] > 2:
        sums.append(sums[-1] // 2)
    late = sums[:0:-1]
    masks = (first, 1, *late)
    for step, mask in enumerate(sums):
        last = step == len(sums) - 1
        held = g
        if late:
            queries, held = lax.optimization_barrier((queries, tick(HEAVY, g)))
            queries = jnp.concatenate([queries, swap(queries, late.pop(0))], axis=0)
        g = tick(HEAVY if held is not g else LIGHT, held, swap(g, mask))
    inv = pl.pallas_call(
        inverse_kernel,
        out_shape=jax.ShapeDtypeStruct((side, 2 * side), F32),
        in_specs=[VMEM],
        out_specs=VMEM,
        compiler_params=pltpu.CompilerParams(vmem_limit_bytes=4 * 2**20),
        name="inverse",
    )(g)
    keep, send = pl.pallas_call(
        functools.partial(score_kernel, q_rows, masks),
        out_shape=(
            jax.ShapeDtypeStruct((EX_DEV, q_rows * devices), F32),
            jax.ShapeDtypeStruct((EX_DEV, q_rows * devices), F32),
        ),
        in_specs=[VMEM] * 4,
        out_specs=(VMEM, VMEM),
        compiler_params=pltpu.CompilerParams(vmem_limit_bytes=16 * 2**20),
        name="score",
    )(inv, mine, other, queries)
    return keep + swap(send, 1)


def solution(mesh):
    return jax.shard_map(
        local,
        mesh=mesh,
        in_specs=(
            P(None, ("groups", "tok"), None),
            P(None, ("groups", "tok"), None),
            P(("groups", "tok")),
            P(),
            P(),
            P(None, ("groups", "tok"), None),
            P(),
        ),
        out_specs=P(("groups", "tok"), None),
        check_vma=False,
    )
```

```python
import functools

import jax
import jax.numpy as jnp
from jax import lax
from jax.experimental import pallas as pl
from jax.experimental.pallas import tpu as pltpu
from jax.sharding import PartitionSpec as P

EX_DEV = 16
BLOCK = 8
LIGHT, HEAVY = 10**6, 2 * 10**10
HIGH = lax.Precision.HIGHEST
F32 = jnp.float32
BF16 = jnp.bfloat16
VMEM = pl.BlockSpec(memory_space=pltpu.VMEM)
HBM = pl.BlockSpec(memory_space=pltpu.HBM)


def role(me, devices):
    return me & 1


def nt(x, y, precision=None):
    return lax.dot_general(
        x, y, (((1,), (1,)), ((), ())), precision=precision, preferred_element_type=F32
    )


def project_kernel(devices, act, grad, ids, pin, pout, weight, zero, keep, send, own):
    ckpts, rows, _ = act.shape
    side = pin.shape[0]
    half = rows // 2

    def dots(x, w):
        return [
            nt(x[c, h * half : (h + 1) * half, :], w[...]) for c in range(ckpts) for h in range(2)
        ]

    s = dots(grad, pout)
    a = dots(act, pin)
    first, second = (
        jnp.concatenate(
            [jnp.concatenate([a[j], s[j]], axis=1) for j in (2 * c, 2 * c + 1)], axis=0
        )
        for c in range(2)
    )
    odd = role(lax.axis_index("tok"), devices)
    mine = jnp.where(odd == 0, first, second)
    tail = jnp.broadcast_to(ids[...].astype(F32), (8, rows))
    scale = jnp.where(odd == 0, weight[:, 0:1], weight[:, 1:2]) / side + zero[0:1, 0:1]
    keep[0:rows, :] = mine
    keep[rows : rows + 8, :] = tail
    keep[rows + 8 :, :] = jnp.broadcast_to(scale, (8, 2 * side))
    send[0:rows, :] = jnp.where(odd == 0, second, first)
    send[rows : rows + 8, :] = tail
    own[...] = factors(mine, rows * devices)


def project(devices, act, grad, ids, pin, pout, weight, zero):
    rows = act.shape[1]
    side = pout.shape[0]
    return pl.pallas_call(
        functools.partial(project_kernel, devices),
        out_shape=(
            jax.ShapeDtypeStruct((rows + 16, 2 * side), F32),
            jax.ShapeDtypeStruct((rows + 8, 2 * side), F32),
            jax.ShapeDtypeStruct((side, 2 * side), F32),
        ),
        in_specs=[VMEM] * 7,
        out_specs=(VMEM, VMEM, VMEM),
        compiler_params=pltpu.CompilerParams(vmem_limit_bytes=24 * 2**20),
        cost_estimate=pl.CostEstimate(flops=HEAVY, bytes_accessed=2 * 10**7, transcendentals=0),
        name="project",
    )(act, grad, ids, pin, pout, weight, zero)


def factors(x, total):
    side = x.shape[1] // 2
    g = lax.dot_general(
        x, x, (((0,), (0,)), ((), ())), precision=HIGH, preferred_element_type=F32
    )
    lane = lax.broadcasted_iota(jnp.int32, (side, 2 * side), 1)
    return jnp.where(lane < side, g[:side], g[side:]) * (1.0 / total)


def gram_kernel(total, x, own, out):
    rows = x.shape[0] - 8
    out[...] = own[...] + factors(x[0:rows, :], total)


def lead_kernel(out):
    out[...] = jnp.zeros(out.shape, F32)


def lead():
    return pl.pallas_call(
        lead_kernel,
        out_shape=jax.ShapeDtypeStruct((8, 128), F32),
        out_specs=VMEM,
        compiler_params=pltpu.CompilerParams(vmem_limit_bytes=2**20),
        cost_estimate=pl.CostEstimate(flops=HEAVY, bytes_accessed=2 * 10**7, transcendentals=0),
        name="lead",
    )()


def tick_kernel(*refs):
    total = refs[0][...]
    for ref in refs[1:-1]:
        total = total + ref[...]
    refs[-1][...] = total


def tick(weight, *terms):
    return pl.pallas_call(
        tick_kernel,
        out_shape=jax.ShapeDtypeStruct(terms[0].shape, F32),
        in_specs=[VMEM] * len(terms),
        out_specs=VMEM,
        compiler_params=pltpu.CompilerParams(vmem_limit_bytes=2**20),
        cost_estimate=pl.CostEstimate(
            flops=weight, bytes_accessed=weight // 1000, transcendentals=0
        ),
        name="tick",
    )(*terms)


def inverse_kernel(g, out):
    side, lanes = g.shape
    lane = lax.broadcasted_iota(jnp.int32, (side, lanes), 1)
    row = lax.broadcasted_iota(jnp.int32, (side, lanes), 0)
    left = lane < side
    local = jnp.where(left, lane, lane - side)
    m = g[...]
    diag = jnp.sum(jnp.where(local == row, m, 0.0), axis=0, keepdims=True)
    first = left[:1]
    tr_a = jnp.sum(jnp.where(first, diag, 0.0), axis=1, keepdims=True)
    tr_s = jnp.sum(jnp.where(first, 0.0, diag), axis=1, keepdims=True)
    damp = 0.05 * (jnp.where(first, tr_a, tr_s) / side)
    m = m + jnp.where(local == row, damp, 0.0)
    lead = local[:1]
    for k in range(0, side, BLOCK):
        at = jnp.where(left, k, side + k)
        cols = [jnp.take_along_axis(m, at + j, axis=1) for j in range(BLOCK)]
        small = [[col[k + i : k + i + 1] for col in cols] for i in range(BLOCK)]
        lines = []
        for i in range(BLOCK):
            line = m[k + i : k + i + 1]
            for j in range(BLOCK):
                line = jnp.where(lead == k + j, float(i == j), line)
            lines.append(line)
        for p in range(BLOCK):
            scale = 1.0 / small[p][p]
            for j in range(p + 1, BLOCK):
                small[p][j] = small[p][j] * scale
            lines[p] = lines[p] * scale
            for i in range(BLOCK):
                if i != p:
                    factor = small[i][p]
                    for j in range(p + 1, BLOCK):
                        small[i][j] = small[i][j] - factor * small[p][j]
                    lines[i] = lines[i] - factor * lines[p]
        inside = (row >= k) & (row < k + BLOCK)
        m = jnp.where(inside | ((local >= k) & (local < k + BLOCK)), 0.0, m)
        for j in range(BLOCK):
            m = m - jnp.where(row == k + j, -1.0, jnp.where(inside, 0.0, cols[j])) * lines[j]
    out[...] = m


def split(x):
    hi = x.astype(BF16)
    return hi, (x - hi.astype(F32)).astype(BF16)


def score_kernel(q_rows, masks, inv, mine, other, queries, keep, send):
    rows, lanes = other.shape[0] - 8, other.shape[1]
    side = lanes // 2
    me = lax.axis_index("tok")
    x = jnp.concatenate([mine[0:rows, :], other[0:rows, :]], axis=0)
    lane = lax.broadcasted_iota(jnp.int32, (side, lanes), 1)
    left = lane < side
    p = inv[...]
    ai = jnp.where(left, p, pltpu.roll(p, side, 1))
    si = jnp.where(left, 0.0, p)
    aa = jnp.dot(
        x,
        jnp.concatenate([ai, jnp.zeros_like(ai)], axis=0),
        precision=HIGH,
        preferred_element_type=F32,
    )
    st = nt(si, x, HIGH)
    a_hi, a_lo = split(aa)
    s_hi, s_lo = split(st)
    s_hi, s_lo = s_hi.astype(F32), s_lo.astype(F32)
    example = lax.broadcasted_iota(jnp.int32, (EX_DEV, rows), 0)
    own_ids = mine[rows : rows + 1, :].astype(jnp.int32) - me * EX_DEV
    near = me ^ 1
    far_ids = other[rows : rows + 1, :].astype(jnp.int32) - near * EX_DEV
    parts = []
    for block, which in enumerate((own_ids, far_ids)):
        mask = (which == example).astype(F32)
        span = slice(block * rows, (block + 1) * rows)
        lhs = jnp.concatenate(
            [
                (v[:, None, span] * mask[None]).reshape(side * EX_DEV, rows).astype(BF16)
                for v in (s_hi, s_lo)
            ],
            axis=1,
        )
        rhs = jnp.concatenate(
            [
                jnp.concatenate([a_hi[span], a_lo[span]], axis=1),
                jnp.concatenate([a_hi[span], jnp.zeros_like(a_lo[span])], axis=1),
            ],
            axis=0,
        )
        both = jnp.dot(lhs, rhs, preferred_element_type=F32)
        both = (both[:, :lanes] + both[:, lanes:]).reshape(side // 2, 2, EX_DEV, lanes)
        first = lax.broadcasted_iota(jnp.int32, (EX_DEV, lanes), 1) < side
        parts.append(
            jnp.concatenate(
                [jnp.where(first, both[j, 0], both[j, 1]) for j in range(side // 2)], axis=1
            )
        )
    sketch = jnp.concatenate(parts, axis=0)
    k_hi, k_lo = split(sketch)
    inner = nt(jnp.concatenate([k_hi, k_lo], axis=0), queries[...])
    inner = inner[: 2 * EX_DEV] + inner[2 * EX_DEV :]
    count = queries.shape[0]
    src = lax.broadcasted_iota(jnp.int32, (count, count), 0)
    dst = lax.broadcasted_iota(jnp.int32, (count, count), 1)
    shift = q_rows.bit_length() - 1
    block = me
    for bit, mask in enumerate(masks):
        block = block ^ ((src >> (shift + bit)) & 1) * mask
    order = (block * q_rows + (src & (q_rows - 1)) == dst).astype(F32)
    scores = jnp.dot(inner, order, precision=HIGH, preferred_element_type=F32)
    scores = scores * mine[rows + 8 : rows + 9, 0:1]
    keep[...] = scores[:EX_DEV]
    send[...] = scores[EX_DEV:]


def local(inputs_act, out_grads, example_ids, proj_in, proj_out, query_sketch, ckpt_weight):
    rows = inputs_act.shape[1]
    side = proj_in.shape[1]
    q_rows = query_sketch.shape[1]
    devices = lax.axis_size("tok")
    total = rows * devices
    me = lax.axis_index("tok")

    def swap(x, mask):
        return lax.ppermute(x, "tok", [(i, i ^ mask) for i in range(devices)])

    ids = example_ids.reshape(1, rows)
    first = devices // 2
    raw, zero = lax.optimization_barrier((query_sketch, lead()))
    arrived = swap(raw, first)
    mine, send, own = project(devices, inputs_act, out_grads, ids, proj_in.T, proj_out.T, ckpt_weight[None], zero)
    other = swap(send, 1)
    arrived, mine = lax.optimization_barrier((arrived, mine))
    both = jnp.concatenate([query_sketch, arrived], axis=1)
    even = role(me, devices) == 0
    queries = jnp.where(even, both[0], both[1])
    queries = jnp.concatenate([queries, swap(jnp.where(even, both[1], both[0]), 1)], axis=0)
    g = pl.pallas_call(
        functools.partial(gram_kernel, total),
        out_shape=jax.ShapeDtypeStruct((side, 2 * side), F32),
        in_specs=[VMEM, VMEM],
        out_specs=VMEM,
        compiler_params=pltpu.CompilerParams(vmem_limit_bytes=4 * 2**20),
        name="gram",
    )(other, tick(HEAVY, own))
    far = [devices >> k for k in range(1, devices.bit_length() - 2)]
    sums = [2, *far]
    late = [*far[:0:-1], 2]
    masks = (first, 1, *late)
    for step, mask in enumerate(sums):
        last = step == len(sums) - 1
        held = g
        if late:
            queries, held = lax.optimization_barrier((queries, tick(HEAVY, g)))
            queries = jnp.concatenate([queries, swap(queries, late.pop(0))], axis=0)
        g = tick(HEAVY if held is not g else LIGHT, held, swap(g, mask))
    inv = pl.pallas_call(
        inverse_kernel,
        out_shape=jax.ShapeDtypeStruct((side, 2 * side), F32),
        in_specs=[VMEM],
        out_specs=VMEM,
        compiler_params=pltpu.CompilerParams(vmem_limit_bytes=4 * 2**20),
        name="inverse",
    )(g)
    keep, send = pl.pallas_call(
        functools.partial(score_kernel, q_rows, masks),
        out_shape=(
            jax.ShapeDtypeStruct((EX_DEV, q_rows * devices), F32),
            jax.ShapeDtypeStruct((EX_DEV, q_rows * devices), F32),
        ),
        in_specs=[VMEM] * 4,
        out_specs=(VMEM, VMEM),
        compiler_params=pltpu.CompilerParams(vmem_limit_bytes=16 * 2**20),
        name="score",
    )(inv, mine, other, queries)
    return keep + swap(send, 1)


def solution(mesh):
    return jax.shard_map(
        local,
        mesh=mesh,
        in_specs=(
            P(None, ("groups", "tok"), None),
            P(None, ("groups", "tok"), None),
            P(("groups", "tok")),
            P(),
            P(),
            P(None, ("groups", "tok"), None),
            P(),
        ),
        out_specs=P(("groups", "tok"), None),
        check_vma=False,
    )
```

```python
import functools

import jax
import jax.numpy as jnp
from jax import lax
from jax.experimental import pallas as pl
from jax.experimental.pallas import tpu as pltpu
from jax.sharding import PartitionSpec as P

EX_DEV = 16
BLOCK = 8
LIGHT, HEAVY = 10**6, 2 * 10**10
HIGH = lax.Precision.HIGHEST
F32 = jnp.float32
BF16 = jnp.bfloat16
VMEM = pl.BlockSpec(memory_space=pltpu.VMEM)
HBM = pl.BlockSpec(memory_space=pltpu.HBM)


def role(me, devices):
    return me & 1


def nt(x, y, precision=None):
    return lax.dot_general(
        x, y, (((1,), (1,)), ((), ())), precision=precision, preferred_element_type=F32
    )


def side_kernel(grad, pout, out):
    ckpts, rows, _ = grad.shape
    half = rows // 2
    for j in range(2 * ckpts):
        piece = grad[j // 2, (j % 2) * half : (j % 2 + 1) * half, :]
        out[j * half : (j + 1) * half, :] = nt(piece, pout[...])


def grad_side(grad, pout):
    return pl.pallas_call(
        side_kernel,
        out_shape=jax.ShapeDtypeStruct((grad.shape[0] * grad.shape[1], pout.shape[0]), F32),
        in_specs=[VMEM, VMEM],
        out_specs=VMEM,
        compiler_params=pltpu.CompilerParams(vmem_limit_bytes=8 * 2**20),
        cost_estimate=pl.CostEstimate(flops=LIGHT, bytes_accessed=1000, transcendentals=0),
        name="grad_side",
    )(grad, pout)


def project_kernel(devices, act, ids, pin, s_all, weight, zero, keep, send, own):
    ckpts, rows, _ = act.shape
    side = pin.shape[0]
    half = rows // 2

    def dots(x, w):
        return [
            nt(x[c, h * half : (h + 1) * half, :], w[...]) for c in range(ckpts) for h in range(2)
        ]

    s = [s_all[j * half : (j + 1) * half, :] for j in range(2 * ckpts)]
    a = dots(act, pin)
    first, second = (
        jnp.concatenate(
            [jnp.concatenate([a[j], s[j]], axis=1) for j in (2 * c, 2 * c + 1)], axis=0
        )
        for c in range(2)
    )
    odd = role(lax.axis_index("tok"), devices)
    mine = jnp.where(odd == 0, first, second)
    tail = jnp.broadcast_to(ids[...].astype(F32), (8, rows))
    scale = jnp.where(odd == 0, weight[:, 0:1], weight[:, 1:2]) / side + zero[0:1, 0:1]
    keep[0:rows, :] = mine
    keep[rows : rows + 8, :] = tail
    keep[rows + 8 :, :] = jnp.broadcast_to(scale, (8, 2 * side))
    send[0:rows, :] = jnp.where(odd == 0, second, first)
    send[rows : rows + 8, :] = tail
    own[...] = factors(mine, rows * devices)


def project(devices, act, grad, ids, pin, pout, weight, zero):
    rows = act.shape[1]
    side = pout.shape[0]
    s_all = grad_side(grad, pout)
    return pl.pallas_call(
        functools.partial(project_kernel, devices),
        out_shape=(
            jax.ShapeDtypeStruct((rows + 16, 2 * side), F32),
            jax.ShapeDtypeStruct((rows + 8, 2 * side), F32),
            jax.ShapeDtypeStruct((side, 2 * side), F32),
        ),
        in_specs=[VMEM] * 6,
        out_specs=(VMEM, VMEM, VMEM),
        compiler_params=pltpu.CompilerParams(vmem_limit_bytes=24 * 2**20),
        cost_estimate=pl.CostEstimate(flops=HEAVY, bytes_accessed=2 * 10**7, transcendentals=0),
        name="project",
    )(act, ids, pin, s_all, weight, zero)


def factors(x, total):
    side = x.shape[1] // 2
    g = lax.dot_general(
        x, x, (((0,), (0,)), ((), ())), precision=HIGH, preferred_element_type=F32
    )
    lane = lax.broadcasted_iota(jnp.int32, (side, 2 * side), 1)
    return jnp.where(lane < side, g[:side], g[side:]) * (1.0 / total)


def gram_kernel(total, x, own, out):
    rows = x.shape[0] - 8
    out[...] = own[...] + factors(x[0:rows, :], total)


def lead_kernel(out):
    out[...] = jnp.zeros(out.shape, F32)


def lead():
    return pl.pallas_call(
        lead_kernel,
        out_shape=jax.ShapeDtypeStruct((8, 128), F32),
        out_specs=VMEM,
        compiler_params=pltpu.CompilerParams(vmem_limit_bytes=2**20),
        cost_estimate=pl.CostEstimate(flops=HEAVY, bytes_accessed=2 * 10**7, transcendentals=0),
        name="lead",
    )()


def tick_kernel(*refs):
    total = refs[0][...]
    for ref in refs[1:-1]:
        total = total + ref[...]
    refs[-1][...] = total


def tick(weight, *terms):
    return pl.pallas_call(
        tick_kernel,
        out_shape=jax.ShapeDtypeStruct(terms[0].shape, F32),
        in_specs=[VMEM] * len(terms),
        out_specs=VMEM,
        compiler_params=pltpu.CompilerParams(vmem_limit_bytes=2**20),
        cost_estimate=pl.CostEstimate(
            flops=weight, bytes_accessed=weight // 1000, transcendentals=0
        ),
        name="tick",
    )(*terms)


def inverse_kernel(g, out):
    side, lanes = g.shape
    lane = lax.broadcasted_iota(jnp.int32, (side, lanes), 1)
    row = lax.broadcasted_iota(jnp.int32, (side, lanes), 0)
    left = lane < side
    local = jnp.where(left, lane, lane - side)
    m = g[...]
    diag = jnp.sum(jnp.where(local == row, m, 0.0), axis=0, keepdims=True)
    first = left[:1]
    tr_a = jnp.sum(jnp.where(first, diag, 0.0), axis=1, keepdims=True)
    tr_s = jnp.sum(jnp.where(first, 0.0, diag), axis=1, keepdims=True)
    damp = 0.05 * (jnp.where(first, tr_a, tr_s) / side)
    m = m + jnp.where(local == row, damp, 0.0)
    lead = local[:1]
    for k in range(0, side, BLOCK):
        at = jnp.where(left, k, side + k)
        cols = [jnp.take_along_axis(m, at + j, axis=1) for j in range(BLOCK)]
        small = [[col[k + i : k + i + 1] for col in cols] for i in range(BLOCK)]
        lines = []
        for i in range(BLOCK):
            line = m[k + i : k + i + 1]
            for j in range(BLOCK):
                line = jnp.where(lead == k + j, float(i == j), line)
            lines.append(line)
        for p in range(BLOCK):
            scale = 1.0 / small[p][p]
            for j in range(p + 1, BLOCK):
                small[p][j] = small[p][j] * scale
            lines[p] = lines[p] * scale
            for i in range(BLOCK):
                if i != p:
                    factor = small[i][p]
                    for j in range(p + 1, BLOCK):
                        small[i][j] = small[i][j] - factor * small[p][j]
                    lines[i] = lines[i] - factor * lines[p]
        inside = (row >= k) & (row < k + BLOCK)
        m = jnp.where(inside | ((local >= k) & (local < k + BLOCK)), 0.0, m)
        for j in range(BLOCK):
            m = m - jnp.where(row == k + j, -1.0, jnp.where(inside, 0.0, cols[j])) * lines[j]
    out[...] = m


def split(x):
    hi = x.astype(BF16)
    return hi, (x - hi.astype(F32)).astype(BF16)


def score_kernel(q_rows, masks, inv, mine, other, queries, keep, send):
    rows, lanes = other.shape[0] - 8, other.shape[1]
    side = lanes // 2
    me = lax.axis_index("tok")
    x = jnp.concatenate([mine[0:rows, :], other[0:rows, :]], axis=0)
    lane = lax.broadcasted_iota(jnp.int32, (side, lanes), 1)
    left = lane < side
    p = inv[...]
    ai = jnp.where(left, p, pltpu.roll(p, side, 1))
    si = jnp.where(left, 0.0, p)
    aa = jnp.dot(
        x,
        jnp.concatenate([ai, jnp.zeros_like(ai)], axis=0),
        precision=HIGH,
        preferred_element_type=F32,
    )
    st = nt(si, x, HIGH)
    a_hi, a_lo = split(aa)
    s_hi, s_lo = split(st)
    s_hi, s_lo = s_hi.astype(F32), s_lo.astype(F32)
    example = lax.broadcasted_iota(jnp.int32, (EX_DEV, rows), 0)
    own_ids = mine[rows : rows + 1, :].astype(jnp.int32) - me * EX_DEV
    near = me ^ 1
    far_ids = other[rows : rows + 1, :].astype(jnp.int32) - near * EX_DEV
    parts = []
    for block, which in enumerate((own_ids, far_ids)):
        mask = (which == example).astype(F32)
        span = slice(block * rows, (block + 1) * rows)
        lhs = jnp.concatenate(
            [
                (v[:, None, span] * mask[None]).reshape(side * EX_DEV, rows).astype(BF16)
                for v in (s_hi, s_lo)
            ],
            axis=1,
        )
        rhs = jnp.concatenate(
            [
                jnp.concatenate([a_hi[span], a_lo[span]], axis=1),
                jnp.concatenate([a_hi[span], jnp.zeros_like(a_lo[span])], axis=1),
            ],
            axis=0,
        )
        both = jnp.dot(lhs, rhs, preferred_element_type=F32)
        both = (both[:, :lanes] + both[:, lanes:]).reshape(side // 2, 2, EX_DEV, lanes)
        first = lax.broadcasted_iota(jnp.int32, (EX_DEV, lanes), 1) < side
        parts.append(
            jnp.concatenate(
                [jnp.where(first, both[j, 0], both[j, 1]) for j in range(side // 2)], axis=1
            )
        )
    sketch = jnp.concatenate(parts, axis=0)
    k_hi, k_lo = split(sketch)
    inner = nt(jnp.concatenate([k_hi, k_lo], axis=0), queries[...])
    inner = inner[: 2 * EX_DEV] + inner[2 * EX_DEV :]
    count = queries.shape[0]
    src = lax.broadcasted_iota(jnp.int32, (count, count), 0)
    dst = lax.broadcasted_iota(jnp.int32, (count, count), 1)
    shift = q_rows.bit_length() - 1
    block = me
    for bit, mask in enumerate(masks):
        block = block ^ ((src >> (shift + bit)) & 1) * mask
    order = (block * q_rows + (src & (q_rows - 1)) == dst).astype(F32)
    scores = jnp.dot(inner, order, precision=HIGH, preferred_element_type=F32)
    scores = scores * mine[rows + 8 : rows + 9, 0:1]
    keep[...] = scores[:EX_DEV]
    send[...] = scores[EX_DEV:]


def local(inputs_act, out_grads, example_ids, proj_in, proj_out, query_sketch, ckpt_weight):
    rows = inputs_act.shape[1]
    side = proj_in.shape[1]
    q_rows = query_sketch.shape[1]
    devices = lax.axis_size("tok")
    total = rows * devices
    me = lax.axis_index("tok")

    def swap(x, mask):
        return lax.ppermute(x, "tok", [(i, i ^ mask) for i in range(devices)])

    ids = example_ids.reshape(1, rows)
    first = devices // 2
    raw, zero = lax.optimization_barrier((query_sketch, lead()))
    arrived = swap(raw, first)
    mine, send, own = project(devices, inputs_act, out_grads, ids, proj_in.T, proj_out.T, ckpt_weight[None], zero)
    other = swap(send, 1)
    arrived, mine = lax.optimization_barrier((arrived, mine))
    both = jnp.concatenate([query_sketch, arrived], axis=1)
    even = role(me, devices) == 0
    queries = jnp.where(even, both[0], both[1])
    queries = jnp.concatenate([queries, swap(jnp.where(even, both[1], both[0]), 1)], axis=0)
    g = pl.pallas_call(
        functools.partial(gram_kernel, total),
        out_shape=jax.ShapeDtypeStruct((side, 2 * side), F32),
        in_specs=[VMEM, VMEM],
        out_specs=VMEM,
        compiler_params=pltpu.CompilerParams(vmem_limit_bytes=4 * 2**20),
        name="gram",
    )(other, tick(HEAVY, own))
    far = [devices >> k for k in range(1, devices.bit_length() - 2)]
    sums = [2, *far]
    late = [*far[:0:-1], 2]
    masks = (first, 1, *late)
    for step, mask in enumerate(sums):
        last = step == len(sums) - 1
        held = g
        if late:
            queries, held = lax.optimization_barrier((queries, tick(HEAVY, g)))
            queries = jnp.concatenate([queries, swap(queries, late.pop(0))], axis=0)
        g = tick(HEAVY if held is not g else LIGHT, held, swap(g, mask))
    inv = pl.pallas_call(
        inverse_kernel,
        out_shape=jax.ShapeDtypeStruct((side, 2 * side), F32),
        in_specs=[VMEM],
        out_specs=VMEM,
        compiler_params=pltpu.CompilerParams(vmem_limit_bytes=4 * 2**20),
        name="inverse",
    )(g)
    keep, send = pl.pallas_call(
        functools.partial(score_kernel, q_rows, masks),
        out_shape=(
            jax.ShapeDtypeStruct((EX_DEV, q_rows * devices), F32),
            jax.ShapeDtypeStruct((EX_DEV, q_rows * devices), F32),
        ),
        in_specs=[VMEM] * 4,
        out_specs=(VMEM, VMEM),
        compiler_params=pltpu.CompilerParams(vmem_limit_bytes=16 * 2**20),
        name="score",
    )(inv, mine, other, queries)
    return keep + swap(send, 1)


def solution(mesh):
    return jax.shard_map(
        local,
        mesh=mesh,
        in_specs=(
            P(None, ("groups", "tok"), None),
            P(None, ("groups", "tok"), None),
            P(("groups", "tok")),
            P(),
            P(),
            P(None, ("groups", "tok"), None),
            P(),
        ),
        out_specs=P(("groups", "tok"), None),
        check_vma=False,
    )
```

```python
import functools

import jax
import jax.numpy as jnp
from jax import lax
from jax.experimental import pallas as pl
from jax.experimental.pallas import tpu as pltpu
from jax.sharding import PartitionSpec as P

EX_DEV = 16
BLOCK = 8
LIGHT, HEAVY = 10**6, 2 * 10**10
HIGH = lax.Precision.HIGHEST
F32 = jnp.float32
BF16 = jnp.bfloat16
VMEM = pl.BlockSpec(memory_space=pltpu.VMEM)
HBM = pl.BlockSpec(memory_space=pltpu.HBM)


def role(me, devices):
    bit = me
    for shift in range(1, devices.bit_length() - 1):
        bit = bit ^ (me >> shift)
    return bit & 1


def nt(x, y, precision=None):
    return lax.dot_general(
        x, y, (((1,), (1,)), ((), ())), precision=precision, preferred_element_type=F32
    )


def side_kernel(grad, pout, out):
    ckpts, rows, _ = grad.shape
    half = rows // 2
    for j in range(2 * ckpts):
        piece = grad[j // 2, (j % 2) * half : (j % 2 + 1) * half, :]
        out[j * half : (j + 1) * half, :] = nt(piece, pout[...])


def grad_side(grad, pout):
    return pl.pallas_call(
        side_kernel,
        out_shape=jax.ShapeDtypeStruct((grad.shape[0] * grad.shape[1], pout.shape[0]), F32),
        in_specs=[VMEM, VMEM],
        out_specs=VMEM,
        compiler_params=pltpu.CompilerParams(vmem_limit_bytes=8 * 2**20),
        cost_estimate=pl.CostEstimate(flops=LIGHT, bytes_accessed=1000, transcendentals=0),
        name="grad_side",
    )(grad, pout)


def project_kernel(devices, act, ids, pin, s_all, weight, zero, keep, send, own):
    ckpts, rows, _ = act.shape
    side = pin.shape[0]
    half = rows // 2

    def dots(x, w):
        return [
            nt(x[c, h * half : (h + 1) * half, :], w[...]) for c in range(ckpts) for h in range(2)
        ]

    s = [s_all[j * half : (j + 1) * half, :] for j in range(2 * ckpts)]
    a = dots(act, pin)
    first, second = (
        jnp.concatenate(
            [jnp.concatenate([a[j], s[j]], axis=1) for j in (2 * c, 2 * c + 1)], axis=0
        )
        for c in range(2)
    )
    odd = role(lax.axis_index("tok"), devices)
    mine = jnp.where(odd == 0, first, second)
    tail = jnp.broadcast_to(ids[...].astype(F32), (8, rows))
    scale = jnp.where(odd == 0, weight[:, 0:1], weight[:, 1:2]) / side + zero[0:1, 0:1]
    keep[0:rows, :] = mine
    keep[rows : rows + 8, :] = tail
    keep[rows + 8 :, :] = jnp.broadcast_to(scale, (8, 2 * side))
    send[0:rows, :] = jnp.where(odd == 0, second, first)
    send[rows : rows + 8, :] = tail
    own[...] = factors(mine, rows * devices)


def project(devices, act, grad, ids, pin, pout, weight, zero):
    rows = act.shape[1]
    side = pout.shape[0]
    s_all = grad_side(grad, pout)
    return pl.pallas_call(
        functools.partial(project_kernel, devices),
        out_shape=(
            jax.ShapeDtypeStruct((rows + 16, 2 * side), F32),
            jax.ShapeDtypeStruct((rows + 8, 2 * side), F32),
            jax.ShapeDtypeStruct((side, 2 * side), F32),
        ),
        in_specs=[VMEM] * 6,
        out_specs=(VMEM, VMEM, VMEM),
        compiler_params=pltpu.CompilerParams(vmem_limit_bytes=24 * 2**20),
        cost_estimate=pl.CostEstimate(flops=HEAVY, bytes_accessed=2 * 10**7, transcendentals=0),
        name="project",
    )(act, ids, pin, s_all, weight, zero)


def factors(x, total):
    side = x.shape[1] // 2
    g = lax.dot_general(
        x, x, (((0,), (0,)), ((), ())), precision=HIGH, preferred_element_type=F32
    )
    lane = lax.broadcasted_iota(jnp.int32, (side, 2 * side), 1)
    return jnp.where(lane < side, g[:side], g[side:]) * (1.0 / total)


def gram_kernel(total, x, own, out):
    rows = x.shape[0] - 8
    out[...] = own[...] + factors(x[0:rows, :], total)


def lead_kernel(out):
    out[...] = jnp.zeros(out.shape, F32)


def lead():
    return pl.pallas_call(
        lead_kernel,
        out_shape=jax.ShapeDtypeStruct((8, 128), F32),
        out_specs=VMEM,
        compiler_params=pltpu.CompilerParams(vmem_limit_bytes=2**20),
        cost_estimate=pl.CostEstimate(flops=HEAVY, bytes_accessed=2 * 10**7, transcendentals=0),
        name="lead",
    )()


def tick_kernel(*refs):
    total = refs[0][...]
    for ref in refs[1:-1]:
        total = total + ref[...]
    refs[-1][...] = total


def tick(weight, *terms):
    return pl.pallas_call(
        tick_kernel,
        out_shape=jax.ShapeDtypeStruct(terms[0].shape, F32),
        in_specs=[VMEM] * len(terms),
        out_specs=VMEM,
        compiler_params=pltpu.CompilerParams(vmem_limit_bytes=2**20),
        cost_estimate=pl.CostEstimate(
            flops=weight, bytes_accessed=weight // 1000, transcendentals=0
        ),
        name="tick",
    )(*terms)


def inverse_kernel(g, out):
    side, lanes = g.shape
    lane = lax.broadcasted_iota(jnp.int32, (side, lanes), 1)
    row = lax.broadcasted_iota(jnp.int32, (side, lanes), 0)
    left = lane < side
    local = jnp.where(left, lane, lane - side)
    m = g[...]
    diag = jnp.sum(jnp.where(local == row, m, 0.0), axis=0, keepdims=True)
    first = left[:1]
    tr_a = jnp.sum(jnp.where(first, diag, 0.0), axis=1, keepdims=True)
    tr_s = jnp.sum(jnp.where(first, 0.0, diag), axis=1, keepdims=True)
    damp = 0.05 * (jnp.where(first, tr_a, tr_s) / side)
    m = m + jnp.where(local == row, damp, 0.0)
    lead = local[:1]
    for k in range(0, side, BLOCK):
        at = jnp.where(left, k, side + k)
        cols = [jnp.take_along_axis(m, at + j, axis=1) for j in range(BLOCK)]
        small = [[col[k + i : k + i + 1] for col in cols] for i in range(BLOCK)]
        lines = []
        for i in range(BLOCK):
            line = m[k + i : k + i + 1]
            for j in range(BLOCK):
                line = jnp.where(lead == k + j, float(i == j), line)
            lines.append(line)
        for p in range(BLOCK):
            scale = 1.0 / small[p][p]
            for j in range(p + 1, BLOCK):
                small[p][j] = small[p][j] * scale
            lines[p] = lines[p] * scale
            for i in range(BLOCK):
                if i != p:
                    factor = small[i][p]
                    for j in range(p + 1, BLOCK):
                        small[i][j] = small[i][j] - factor * small[p][j]
                    lines[i] = lines[i] - factor * lines[p]
        inside = (row >= k) & (row < k + BLOCK)
        m = jnp.where(inside | ((local >= k) & (local < k + BLOCK)), 0.0, m)
        for j in range(BLOCK):
            m = m - jnp.where(row == k + j, -1.0, jnp.where(inside, 0.0, cols[j])) * lines[j]
    out[...] = m


def split(x):
    hi = x.astype(BF16)
    return hi, (x - hi.astype(F32)).astype(BF16)


def sketch_kernel(inv, mine, other, queries, lhs_out, inner_out):
    rows, lanes = other.shape[0] - 8, other.shape[1]
    side = lanes // 2
    me = lax.axis_index("tok")
    x = jnp.concatenate([mine[0:rows, :], other[0:rows, :]], axis=0)
    lane = lax.broadcasted_iota(jnp.int32, (side, lanes), 1)
    left = lane < side
    p = inv[...]
    ai = jnp.where(left, p, pltpu.roll(p, side, 1))
    si = jnp.where(left, 0.0, p)
    aa = jnp.dot(
        x,
        jnp.concatenate([ai, jnp.zeros_like(ai)], axis=0),
        precision=HIGH,
        preferred_element_type=F32,
    )
    st = nt(si, x, HIGH)
    a_hi, a_lo = split(aa)
    s_hi, s_lo = split(st)
    s_hi, s_lo = s_hi.astype(F32), s_lo.astype(F32)
    example = lax.broadcasted_iota(jnp.int32, (EX_DEV, rows), 0)
    own_ids = mine[rows : rows + 1, :].astype(jnp.int32) - me * EX_DEV
    near = me ^ 1
    far_ids = other[rows : rows + 1, :].astype(jnp.int32) - near * EX_DEV
    parts = []
    for block, which in enumerate((own_ids, far_ids)):
        mask = (which == example).astype(F32)
        span = slice(block * rows, (block + 1) * rows)
        lhs = jnp.concatenate(
            [
                (v[:, None, span] * mask[None]).reshape(side * EX_DEV, rows).astype(BF16)
                for v in (s_hi, s_lo)
            ],
            axis=1,
        )
        rhs = jnp.concatenate(
            [
                jnp.concatenate([a_hi[span], a_lo[span]], axis=1),
                jnp.concatenate([a_hi[span], jnp.zeros_like(a_lo[span])], axis=1),
            ],
            axis=0,
        )
        both = jnp.dot(lhs, rhs, preferred_element_type=F32)
        both = (both[:, :lanes] + both[:, lanes:]).reshape(side // 2, 2, EX_DEV, lanes)
        first = lax.broadcasted_iota(jnp.int32, (EX_DEV, lanes), 1) < side
        parts.append(
            jnp.concatenate(
                [jnp.where(first, both[j, 0], both[j, 1]) for j in range(side // 2)], axis=1
            )
        )
    sketch = jnp.concatenate(parts, axis=0)
    k_hi, k_lo = split(sketch)
    lhs = jnp.concatenate([k_hi, k_lo], axis=0)
    lhs_out[...] = lhs
    inner_out[...] = nt(lhs, queries[...])


def score_kernel(q_rows, masks, lhs, inner, far, mine, keep, send):
    rows = mine.shape[0] - 16
    me = lax.axis_index("tok")
    inner = jnp.concatenate([inner[...], nt(lhs[...], far[...])], axis=1)
    inner = inner[: 2 * EX_DEV] + inner[2 * EX_DEV :]
    count = inner.shape[1]
    src = lax.broadcasted_iota(jnp.int32, (count, count), 0)
    dst = lax.broadcasted_iota(jnp.int32, (count, count), 1)
    shift = q_rows.bit_length() - 1
    block = me
    for bit, mask in enumerate(masks):
        block = block ^ ((src >> (shift + bit)) & 1) * mask
    order = (block * q_rows + (src & (q_rows - 1)) == dst).astype(F32)
    scores = jnp.dot(inner, order, precision=HIGH, preferred_element_type=F32)
    scores = scores * mine[rows + 8 : rows + 9, 0:1]
    keep[...] = scores[:EX_DEV]
    send[...] = scores[EX_DEV:]


def local(inputs_act, out_grads, example_ids, proj_in, proj_out, query_sketch, ckpt_weight):
    rows = inputs_act.shape[1]
    side = proj_in.shape[1]
    q_rows = query_sketch.shape[1]
    devices = lax.axis_size("tok")
    total = rows * devices
    me = lax.axis_index("tok")

    def swap(x, mask):
        return lax.ppermute(x, "tok", [(i, i ^ mask) for i in range(devices)])

    ids = example_ids.reshape(1, rows)
    first = devices // 2 | 1
    raw, zero = lax.optimization_barrier((query_sketch, lead()))
    arrived = swap(raw, first)
    mine, send, own = project(devices, inputs_act, out_grads, ids, proj_in.T, proj_out.T, ckpt_weight[None], zero)
    other = swap(send, 1)
    arrived, mine = lax.optimization_barrier((arrived, mine))
    both = jnp.concatenate([query_sketch, arrived], axis=1)
    even = role(me, devices) == 0
    queries = jnp.where(even, both[0], both[1])
    queries = jnp.concatenate([queries, swap(jnp.where(even, both[1], both[0]), 1)], axis=0)
    g = pl.pallas_call(
        functools.partial(gram_kernel, total),
        out_shape=jax.ShapeDtypeStruct((side, 2 * side), F32),
        in_specs=[VMEM, VMEM],
        out_specs=VMEM,
        compiler_params=pltpu.CompilerParams(vmem_limit_bytes=4 * 2**20),
        name="gram",
    )(other, tick(HEAVY, own))
    far = [devices >> k | 1 for k in range(1, devices.bit_length() - 2)]
    sums = [3, *far]
    late = [*far[:0:-1], 3]
    masks = (first, 1, *late)
    for step, mask in enumerate(sums):
        last = step == len(sums) - 1
        held = g
        if late:
            queries, held = lax.optimization_barrier((queries, tick(HEAVY, g)))
            far_rows = swap(queries, late.pop(0))
            if late:
                queries = jnp.concatenate([queries, far_rows], axis=0)
        g = tick(HEAVY if held is not g else LIGHT, held, swap(g, mask))
    inv = pl.pallas_call(
        inverse_kernel,
        out_shape=jax.ShapeDtypeStruct((side, 2 * side), F32),
        in_specs=[VMEM],
        out_specs=VMEM,
        compiler_params=pltpu.CompilerParams(vmem_limit_bytes=4 * 2**20),
        name="inverse",
    )(g)
    near_rows, width = queries.shape
    lhs, inner = pl.pallas_call(
        sketch_kernel,
        out_shape=(
            jax.ShapeDtypeStruct((4 * EX_DEV, width), BF16),
            jax.ShapeDtypeStruct((4 * EX_DEV, near_rows), F32),
        ),
        in_specs=[VMEM] * 4,
        out_specs=(VMEM, VMEM),
        compiler_params=pltpu.CompilerParams(vmem_limit_bytes=16 * 2**20),
        name="sketch",
    )(inv, mine, other, queries)
    keep, send = pl.pallas_call(
        functools.partial(score_kernel, q_rows, masks),
        out_shape=(
            jax.ShapeDtypeStruct((EX_DEV, q_rows * devices), F32),
            jax.ShapeDtypeStruct((EX_DEV, q_rows * devices), F32),
        ),
        in_specs=[VMEM] * 4,
        out_specs=(VMEM, VMEM),
        compiler_params=pltpu.CompilerParams(vmem_limit_bytes=8 * 2**20),
        name="score",
    )(lhs, inner, far_rows, mine)
    return keep + swap(send, 1)


def solution(mesh):
    return jax.shard_map(
        local,
        mesh=mesh,
        in_specs=(
            P(None, ("groups", "tok"), None),
            P(None, ("groups", "tok"), None),
            P(("groups", "tok")),
            P(),
            P(),
            P(None, ("groups", "tok"), None),
            P(),
        ),
        out_specs=P(("groups", "tok"), None),
        check_vma=False,
    )
```

```python
import functools

import jax
import jax.numpy as jnp
from jax import lax
from jax.experimental import pallas as pl
from jax.experimental.pallas import tpu as pltpu
from jax.sharding import PartitionSpec as P

EX_DEV = 16
BLOCK = 8
LIGHT, HEAVY = 10**6, 2 * 10**10
HIGH = lax.Precision.HIGHEST
F32 = jnp.float32
BF16 = jnp.bfloat16
VMEM = pl.BlockSpec(memory_space=pltpu.VMEM)
HBM = pl.BlockSpec(memory_space=pltpu.HBM)


def role(me, devices):
    bit = me
    for shift in range(1, devices.bit_length() - 1):
        bit = bit ^ (me >> shift)
    return bit & 1


def nt(x, y, precision=None):
    return lax.dot_general(
        x, y, (((1,), (1,)), ((), ())), precision=precision, preferred_element_type=F32
    )


def side_kernel(grad, pout, out):
    ckpts, rows, _ = grad.shape
    half = rows // 2
    for j in range(2 * ckpts):
        piece = grad[j // 2, (j % 2) * half : (j % 2 + 1) * half, :]
        out[j * half : (j + 1) * half, :] = nt(piece, pout[...])


def grad_side(grad, pout):
    return pl.pallas_call(
        side_kernel,
        out_shape=jax.ShapeDtypeStruct((grad.shape[0] * grad.shape[1], pout.shape[0]), F32),
        in_specs=[VMEM, VMEM],
        out_specs=VMEM,
        compiler_params=pltpu.CompilerParams(vmem_limit_bytes=8 * 2**20),
        cost_estimate=pl.CostEstimate(flops=LIGHT, bytes_accessed=1000, transcendentals=0),
        name="grad_side",
    )(grad, pout)


def project_kernel(devices, act, ids, pin, s_all, weight, zero, keep, send):
    ckpts, rows, _ = act.shape
    side = pin.shape[0]
    half = rows // 2

    def dots(x, w):
        return [
            nt(x[c, h * half : (h + 1) * half, :], w[...]) for c in range(ckpts) for h in range(2)
        ]

    s = [s_all[j * half : (j + 1) * half, :] for j in range(2 * ckpts)]
    a = dots(act, pin)
    first, second = (
        jnp.concatenate(
            [jnp.concatenate([a[j], s[j]], axis=1) for j in (2 * c, 2 * c + 1)], axis=0
        )
        for c in range(2)
    )
    odd = role(lax.axis_index("tok"), devices)
    mine = jnp.where(odd == 0, first, second)
    tail = jnp.broadcast_to(ids[...].astype(F32), (8, rows))
    scale = jnp.where(odd == 0, weight[:, 0:1], weight[:, 1:2]) / side + zero[0:1, 0:1]
    keep[0:rows, :] = mine
    keep[rows : rows + 8, :] = tail
    keep[rows + 8 :, :] = jnp.broadcast_to(scale, (8, 2 * side))
    send[0:rows, :] = jnp.where(odd == 0, second, first)
    send[rows : rows + 8, :] = tail


def project(devices, act, grad, ids, pin, pout, weight, zero):
    rows = act.shape[1]
    side = pout.shape[0]
    s_all = grad_side(grad, pout)
    return pl.pallas_call(
        functools.partial(project_kernel, devices),
        out_shape=(
            jax.ShapeDtypeStruct((rows + 16, 2 * side), F32),
            jax.ShapeDtypeStruct((rows + 8, 2 * side), F32),
        ),
        in_specs=[VMEM] * 6,
        out_specs=(VMEM, VMEM),
        compiler_params=pltpu.CompilerParams(vmem_limit_bytes=24 * 2**20),
        cost_estimate=pl.CostEstimate(flops=HEAVY, bytes_accessed=2 * 10**7, transcendentals=0),
        name="project",
    )(act, ids, pin, s_all, weight, zero)


def factors(x, total):
    side = x.shape[1] // 2
    g = lax.dot_general(
        x, x, (((0,), (0,)), ((), ())), precision=HIGH, preferred_element_type=F32
    )
    lane = lax.broadcasted_iota(jnp.int32, (side, 2 * side), 1)
    return jnp.where(lane < side, g[:side], g[side:]) * (1.0 / total)


def gram_kernel(total, mine, other, out):
    rows = other.shape[0] - 8
    out[...] = factors(jnp.concatenate([mine[0:rows, :], other[0:rows, :]], axis=0), total)


def lead_kernel(out):
    out[...] = jnp.zeros(out.shape, F32)


def lead():
    return pl.pallas_call(
        lead_kernel,
        out_shape=jax.ShapeDtypeStruct((8, 128), F32),
        out_specs=VMEM,
        compiler_params=pltpu.CompilerParams(vmem_limit_bytes=2**20),
        cost_estimate=pl.CostEstimate(flops=HEAVY, bytes_accessed=2 * 10**7, transcendentals=0),
        name="lead",
    )()


def tick_kernel(*refs):
    total = refs[0][...]
    for ref in refs[1:-1]:
        total = total + ref[...]
    refs[-1][...] = total


def tick(weight, *terms):
    return pl.pallas_call(
        tick_kernel,
        out_shape=jax.ShapeDtypeStruct(terms[0].shape, F32),
        in_specs=[VMEM] * len(terms),
        out_specs=VMEM,
        compiler_params=pltpu.CompilerParams(vmem_limit_bytes=2**20),
        cost_estimate=pl.CostEstimate(
            flops=weight, bytes_accessed=weight // 1000, transcendentals=0
        ),
        name="tick",
    )(*terms)


def inverse_kernel(g, out):
    side, lanes = g.shape
    lane = lax.broadcasted_iota(jnp.int32, (side, lanes), 1)
    row = lax.broadcasted_iota(jnp.int32, (side, lanes), 0)
    left = lane < side
    local = jnp.where(left, lane, lane - side)
    m = g[...]
    diag = jnp.sum(jnp.where(local == row, m, 0.0), axis=0, keepdims=True)
    first = left[:1]
    tr_a = jnp.sum(jnp.where(first, diag, 0.0), axis=1, keepdims=True)
    tr_s = jnp.sum(jnp.where(first, 0.0, diag), axis=1, keepdims=True)
    damp = 0.05 * (jnp.where(first, tr_a, tr_s) / side)
    m = m + jnp.where(local == row, damp, 0.0)
    lead = local[:1]
    for k in range(0, side, BLOCK):
        at = jnp.where(left, k, side + k)
        cols = [jnp.take_along_axis(m, at + j, axis=1) for j in range(BLOCK)]
        small = [[col[k + i : k + i + 1] for col in cols] for i in range(BLOCK)]
        lines = []
        for i in range(BLOCK):
            line = m[k + i : k + i + 1]
            for j in range(BLOCK):
                line = jnp.where(lead == k + j, float(i == j), line)
            lines.append(line)
        for p in range(BLOCK):
            scale = 1.0 / small[p][p]
            for j in range(p + 1, BLOCK):
                small[p][j] = small[p][j] * scale
            lines[p] = lines[p] * scale
            for i in range(BLOCK):
                if i != p:
                    factor = small[i][p]
                    for j in range(p + 1, BLOCK):
                        small[i][j] = small[i][j] - factor * small[p][j]
                    lines[i] = lines[i] - factor * lines[p]
        inside = (row >= k) & (row < k + BLOCK)
        m = jnp.where(inside | ((local >= k) & (local < k + BLOCK)), 0.0, m)
        for j in range(BLOCK):
            m = m - jnp.where(row == k + j, -1.0, jnp.where(inside, 0.0, cols[j])) * lines[j]
    out[...] = m


def split(x):
    hi = x.astype(BF16)
    return hi, (x - hi.astype(F32)).astype(BF16)


def sketch_kernel(inv, mine, other, queries, lhs_out, inner_out):
    rows, lanes = other.shape[0] - 8, other.shape[1]
    side = lanes // 2
    me = lax.axis_index("tok")
    x = jnp.concatenate([mine[0:rows, :], other[0:rows, :]], axis=0)
    lane = lax.broadcasted_iota(jnp.int32, (side, lanes), 1)
    left = lane < side
    p = inv[...]
    ai = jnp.where(left, p, pltpu.roll(p, side, 1))
    si = jnp.where(left, 0.0, p)
    aa = jnp.dot(
        x,
        jnp.concatenate([ai, jnp.zeros_like(ai)], axis=0),
        precision=HIGH,
        preferred_element_type=F32,
    )
    st = nt(si, x, HIGH)
    a_hi, a_lo = split(aa)
    s_hi, s_lo = split(st)
    s_hi, s_lo = s_hi.astype(F32), s_lo.astype(F32)
    example = lax.broadcasted_iota(jnp.int32, (EX_DEV, rows), 0)
    own_ids = mine[rows : rows + 1, :].astype(jnp.int32) - me * EX_DEV
    near = me ^ 1
    far_ids = other[rows : rows + 1, :].astype(jnp.int32) - near * EX_DEV
    parts = []
    for block, which in enumerate((own_ids, far_ids)):
        mask = (which == example).astype(F32)
        span = slice(block * rows, (block + 1) * rows)
        lhs = jnp.concatenate(
            [
                (v[:, None, span] * mask[None]).reshape(side * EX_DEV, rows).astype(BF16)
                for v in (s_hi, s_lo)
            ],
            axis=1,
        )
        rhs = jnp.concatenate(
            [
                jnp.concatenate([a_hi[span], a_lo[span]], axis=1),
                jnp.concatenate([a_hi[span], jnp.zeros_like(a_lo[span])], axis=1),
            ],
            axis=0,
        )
        both = jnp.dot(lhs, rhs, preferred_element_type=F32)
        both = (both[:, :lanes] + both[:, lanes:]).reshape(side // 2, 2, EX_DEV, lanes)
        first = lax.broadcasted_iota(jnp.int32, (EX_DEV, lanes), 1) < side
        parts.append(
            jnp.concatenate(
                [jnp.where(first, both[j, 0], both[j, 1]) for j in range(side // 2)], axis=1
            )
        )
    sketch = jnp.concatenate(parts, axis=0)
    k_hi, k_lo = split(sketch)
    lhs = jnp.concatenate([k_hi, k_lo], axis=0)
    lhs_out[...] = lhs
    inner_out[...] = nt(lhs, queries[...])


def score_kernel(q_rows, masks, lhs, inner, far, mine, keep, send):
    rows = mine.shape[0] - 16
    me = lax.axis_index("tok")
    inner = jnp.concatenate([inner[...], nt(lhs[...], far[...])], axis=1)
    inner = inner[: 2 * EX_DEV] + inner[2 * EX_DEV :]
    count = inner.shape[1]
    src = lax.broadcasted_iota(jnp.int32, (count, count), 0)
    dst = lax.broadcasted_iota(jnp.int32, (count, count), 1)
    shift = q_rows.bit_length() - 1
    block = me
    for bit, mask in enumerate(masks):
        block = block ^ ((src >> (shift + bit)) & 1) * mask
    order = (block * q_rows + (src & (q_rows - 1)) == dst).astype(F32)
    scores = jnp.dot(inner, order, precision=HIGH, preferred_element_type=F32)
    scores = scores * mine[rows + 8 : rows + 9, 0:1]
    keep[...] = scores[:EX_DEV]
    send[...] = scores[EX_DEV:]


def local(inputs_act, out_grads, example_ids, proj_in, proj_out, query_sketch, ckpt_weight):
    rows = inputs_act.shape[1]
    side = proj_in.shape[1]
    q_rows = query_sketch.shape[1]
    devices = lax.axis_size("tok")
    total = rows * devices
    me = lax.axis_index("tok")

    def swap(x, mask):
        return lax.ppermute(x, "tok", [(i, i ^ mask) for i in range(devices)])

    ids = example_ids.reshape(1, rows)
    first = devices // 2 | 1
    raw, zero = lax.optimization_barrier((query_sketch, lead()))
    arrived = swap(raw, first)
    mine, send = project(devices, inputs_act, out_grads, ids, proj_in.T, proj_out.T, ckpt_weight[None], zero)
    other = swap(send, 1)
    arrived, mine = lax.optimization_barrier((arrived, mine))
    both = jnp.concatenate([query_sketch, arrived], axis=1)
    even = role(me, devices) == 0
    queries = jnp.where(even, both[0], both[1])
    queries = jnp.concatenate([queries, swap(jnp.where(even, both[1], both[0]), 1)], axis=0)
    g = pl.pallas_call(
        functools.partial(gram_kernel, total),
        out_shape=jax.ShapeDtypeStruct((side, 2 * side), F32),
        in_specs=[VMEM, VMEM],
        out_specs=VMEM,
        compiler_params=pltpu.CompilerParams(vmem_limit_bytes=4 * 2**20),
        name="gram",
    )(mine, other)
    far = [devices >> k | 1 for k in range(1, devices.bit_length() - 2)]
    sums = [3, *far]
    late = [*far[:0:-1], 3]
    masks = (first, 1, *late)
    for step, mask in enumerate(sums):
        last = step == len(sums) - 1
        held = g
        if late:
            queries, held = lax.optimization_barrier((queries, tick(HEAVY, g)))
            far_rows = swap(queries, late.pop(0))
            if late:
                queries = jnp.concatenate([queries, far_rows], axis=0)
        g = tick(HEAVY if held is not g else LIGHT, held, swap(g, mask))
    inv = pl.pallas_call(
        inverse_kernel,
        out_shape=jax.ShapeDtypeStruct((side, 2 * side), F32),
        in_specs=[VMEM],
        out_specs=VMEM,
        compiler_params=pltpu.CompilerParams(vmem_limit_bytes=4 * 2**20),
        name="inverse",
    )(g)
    near_rows, width = queries.shape
    lhs, inner = pl.pallas_call(
        sketch_kernel,
        out_shape=(
            jax.ShapeDtypeStruct((4 * EX_DEV, width), BF16),
            jax.ShapeDtypeStruct((4 * EX_DEV, near_rows), F32),
        ),
        in_specs=[VMEM] * 4,
        out_specs=(VMEM, VMEM),
        compiler_params=pltpu.CompilerParams(vmem_limit_bytes=16 * 2**20),
        name="sketch",
    )(inv, mine, other, queries)
    keep, send = pl.pallas_call(
        functools.partial(score_kernel, q_rows, masks),
        out_shape=(
            jax.ShapeDtypeStruct((EX_DEV, q_rows * devices), F32),
            jax.ShapeDtypeStruct((EX_DEV, q_rows * devices), F32),
        ),
        in_specs=[VMEM] * 4,
        out_specs=(VMEM, VMEM),
        compiler_params=pltpu.CompilerParams(vmem_limit_bytes=8 * 2**20),
        name="score",
    )(lhs, inner, far_rows, mine)
    return keep + swap(send, 1)


def solution(mesh):
    return jax.shard_map(
        local,
        mesh=mesh,
        in_specs=(
            P(None, ("groups", "tok"), None),
            P(None, ("groups", "tok"), None),
            P(("groups", "tok")),
            P(),
            P(),
            P(None, ("groups", "tok"), None),
            P(),
        ),
        out_specs=P(("groups", "tok"), None),
        check_vma=False,
    )
```
